32 devices in a mesh: groups: 2 (over x), pts: 8 (over z, y), ctr: 2 (over core).
Axes of the slice: x: 2, y: 2, z: 4, core: 2. Of those that a mesh axis runs over, the one named last changes fastest.
Arguments:
- points: bfloat16 [32768, 256], P(('groups', 'pts')), parts along dimension 0, may hold values from -2 to 2
- targets: float32 [32768, 128], P(('groups', 'pts')), parts along dimension 0, may hold values from -12 to 12
- centres: bfloat16 [1536, 256], P(('groups', 'ctr')), parts along dimension 0, may hold values from -1 to 1
Outputs:
- solution: float32 [1536, 128], P(('groups', 'ctr')), parts along dimension 0
- fitted: float32 [32768, 128], P(('groups', 'pts')), parts along dimension 0
The draws below stay inside these ranges and needn't reach their ends.
There are 2 independent parts, one for each index of `groups`. The reference program is written for one: setup_inputs(seed, part) draws one part's arguments, and reference() takes and returns one part's arrays. A program takes and returns all parts, laid end to end along the dimension named above; each array names one. Nothing has to cross between parts.
All inputs are finite; a program needn't handle non-finite values.
Results may differ from the reference program's by a relative error of at most 0.0003.
Values may be sent and summed in bfloat16 or wider, within the bound.
A program may use at most 128 MiB of HBM per device.

```python
import math
import jax
import jax.numpy as jnp
from jax import lax

D = 256
OUTS = 128
ITERS = 3
M = 768
N = 16384


NOISE_VAR = 0.17


def centre_table(key):
    normal_part = jax.random.truncated_normal(jax.random.fold_in(key, 11), -4.0, 4.0, (M, D), jnp.float32)
    return normal_part / math.sqrt(D)


def draw_centres(key, part):
    table = centre_table(key)
    return table.astype(jnp.bfloat16)


def draw_points(key, part):
    table = centre_table(key)
    key = jax.random.fold_in(key, 2)
    owners = jax.random.randint(jax.random.fold_in(key, 1), (N,), 0, M)
    spread = jnp.exp(jax.random.uniform(jax.random.fold_in(key, 2), (N, 1), jnp.float32, math.log(0.7), math.log(1.4)))
    normal_noise = jax.random.truncated_normal(jax.random.fold_in(key, 3), -4.0, 4.0, (N, D), jnp.float32)
    noise = normal_noise * spread * math.sqrt(NOISE_VAR / D)
    return (table[owners] + noise).astype(jnp.bfloat16)


def steps_of(stream_key, extent, pieces, smallest, largest):
    factor_of, own = 1.0, jax.random.fold_in(stream_key, 6)
    for dim, shards_of in pieces:
        steps = jnp.exp(jax.random.uniform(jax.random.fold_in(own, dim), (shards_of,), jnp.float32, smallest / len(pieces), largest / len(pieces)))
        factor_of = factor_of * jnp.repeat(steps, extent[dim] // shards_of).reshape([-1 if axis == dim else 1 for axis in range(len(extent))])
    return factor_of


def bell_draw(key, extent, width, bound, cuts=(), kind=jnp.bfloat16):
    result = jax.random.normal(key, extent, jnp.float32) * width
    if len(cuts) > 0:
        result = steps_of(key, extent, cuts, -0.22, 0.18) * result
    return jnp.clip(result, min=-bound, max=bound).astype(kind)


def setup_inputs(seed: int = 0, part: int = 0) -> dict:
    keys = jax.random.split(jax.random.key(seed), 4)
    part_splits = jax.random.split(jax.random.fold_in(keys[3], part), 4)
    return {
        "points": draw_points(jax.random.fold_in(jax.random.fold_in(keys[3], part), 71), part),
        "targets": bell_draw(part_splits[1], (N, OUTS), 3.0, 12.0, ((0, 8),), jnp.float32),
        "centres": draw_centres(jax.random.fold_in(jax.random.fold_in(keys[3], part), 71), part),
    }


GAMMA = 3.0
PENALTY = 0.001
PRECISE = lax.Precision.HIGHEST

def precise_dot(left, right):
    return jnp.dot(left.astype(jnp.float32), right.astype(jnp.float32), precision=PRECISE, preferred_element_type=jnp.float32)

def square_norms(row_set):
    widened = row_set.astype(jnp.float32)
    return lax.optimization_barrier(jnp.sum(widened * widened, axis=1))

def kernel_block(row_set, col_set, col_norms):
    inner_prod = jnp.dot(row_set.astype(jnp.float32), col_set.T.astype(jnp.float32), preferred_element_type=jnp.float32)
    row_norms = square_norms(row_set)
    return jnp.exp(-GAMMA * (row_norms[:, None] + col_norms[None, :] - 2.0 * inner_prod))

def factors(centres):
    centre_count = centres.shape[0]
    gram_matrix = kernel_block(centres, centres, square_norms(centres))
    lower_one = jnp.linalg.cholesky(gram_matrix)
    identity = jnp.eye(centre_count, dtype=jnp.float32)
    shifted = precise_dot(lower_one.T, lower_one) / centre_count + PENALTY * identity
    lower_two = jnp.linalg.cholesky(shifted)
    inverse_one = jax.scipy.linalg.solve_triangular(lower_one, identity, lower=True)
    inverse_two = jax.scipy.linalg.solve_triangular(lower_two, identity, lower=True)
    return (inverse_one, inverse_two)

def reference(points, targets, centres):
    inverse_one, inverse_two = factors(centres)
    scaling = 1.0 / math.sqrt(N)
    col_norms = square_norms(centres)
    block_rows = math.gcd(N, 4096)
    blocks = points.reshape(-1, block_rows, D)
    label_blocks = targets.reshape(-1, block_rows, OUTS)

    def apply_right(matrix):
        return precise_dot(inverse_one.T, precise_dot(inverse_two.T, matrix)) * scaling

    def apply_left(matrix):
        return precise_dot(inverse_two, precise_dot(inverse_one, matrix)) * scaling

    def damping_term(matrix):
        return PENALTY * precise_dot(inverse_two, precise_dot(inverse_two.T, matrix))

    def gram_pass(weights):

        def advance(running, row_block):
            kernel_tile = kernel_block(row_block, centres, col_norms)
            return (running + precise_dot(kernel_tile.T, precise_dot(kernel_tile, weights)), None)
        total, _ = lax.scan(advance, jnp.zeros((M, OUTS), jnp.float32), blocks)
        return total

    def label_pass(running, paired):
        kernel_tile = kernel_block(paired[0], centres, col_norms)
        return (running + precise_dot(kernel_tile.T, paired[1]), None)
    right_side, _ = lax.scan(label_pass, jnp.zeros((M, OUTS), jnp.float32), (blocks, label_blocks))
    residual = apply_left(right_side)
    direction = residual
    solution = jnp.zeros((M, OUTS), jnp.float32)
    sq_now = lax.optimization_barrier(jnp.sum(residual * residual, axis=0))
    for iteration in range(ITERS):
        image = apply_left(gram_pass(apply_right(direction))) + damping_term(direction)
        step_size = sq_now / lax.optimization_barrier(jnp.sum(direction * image, axis=0))
        solution = solution + step_size * direction
        residual = residual - step_size * image
        sq_next = lax.optimization_barrier(jnp.sum(residual * residual, axis=0))
        direction = residual + sq_next / sq_now * direction
        sq_now = sq_next
    weights = apply_right(solution)
    fitted = lax.map(lambda row_block: precise_dot(kernel_block(row_block, centres, col_norms), weights), blocks)
    return (solution, fitted.reshape(N, OUTS))
```

```python
import math

import jax
import jax.numpy as jnp
from jax import lax
from jax.experimental import pallas as pl
from jax.experimental.pallas import tpu as pltpu
from jax.sharding import PartitionSpec as P

ITERS = 3
GAMMA = 3.0
PENALTY = 0.001
BLOCK = 128
PANEL = 8


def split_dot(left, right):
    return jnp.dot(left, right, precision=lax.Precision.HIGH, preferred_element_type=jnp.float32)


def square_norms(row_set):
    widened = row_set.astype(jnp.float32)
    return jnp.sum(widened * widened, axis=1)


def kernel_block(row_set, col_set, col_norms):
    inner_prod = jnp.dot(row_set, col_set.T, preferred_element_type=jnp.float32)
    row_norms = square_norms(row_set)
    return jnp.exp(-GAMMA * (row_norms[:, None] + col_norms[None, :] - 2.0 * inner_prod))


def halves(value):
    high = value.astype(jnp.bfloat16)
    return high, (value - high.astype(jnp.float32)).astype(jnp.bfloat16)


def three_dot(left, right, left_dim, right_dim):
    dims = (((left_dim,), (right_dim,)), ((), ()))

    def one(a, b):
        return lax.dot_general(a, b, dims, preferred_element_type=jnp.float32)

    return one(left[0], right[0]) + (one(left[0], right[1]) + one(left[1], right[0]))


def block_inverse(mixed):
    size = mixed.shape[0]
    lanes = lax.broadcasted_iota(jnp.int32, (PANEL, size), 1)
    rows = lax.broadcasted_iota(jnp.int32, (PANEL, size), 0)
    finished = []
    rest = mixed
    for start in range(0, size, PANEL):
        panel = rest[:PANEL]
        below = rest[PANEL:]
        count = below.shape[0]
        cols = [
            jnp.broadcast_to(panel[:, start + c : start + c + 1], (PANEL, size)) for c in range(PANEL)
        ]
        if count:
            lows = [
                jnp.broadcast_to(below[:, start + c : start + c + 1], (count, size)) for c in range(PANEL)
            ]
            below_lanes = lax.broadcasted_iota(jnp.int32, (count, size), 1)
            inside = (below_lanes >= start) & (below_lanes < start + PANEL)
            below = jnp.where(inside, 0.0, below)
        inside_panel = (lanes >= start) & (lanes < start + PANEL)
        panel = jnp.where(inside_panel, jnp.where(lanes - start == rows, 1.0, 0.0), panel)
        for c in range(PANEL):
            root = lax.rsqrt(cols[c][c : c + 1])
            scaled = panel[c : c + 1] * root
            lower = jnp.where(rows > c, cols[c] * root, 0.0)
            panel = jnp.where(rows == c, scaled, panel - lower * scaled)
            if count:
                low = lows[c] * root
                below = below - low * scaled
            for later in range(c + 1, PANEL):
                factor = cols[later][c : c + 1] * root
                cols[later] = cols[later] - lower * factor
                if count:
                    lows[later] = lows[later] - low * factor
        finished.append(jnp.where(lanes < start + PANEL, panel, 0.0))
        rest = below
    return jnp.concatenate(finished, axis=0)


def inverse_kernel(matrix_ref, inverse_ref, work):
    total = matrix_ref.shape[0]
    blocks = total // BLOCK
    work[...] = matrix_ref[...]
    row_ids = lax.broadcasted_iota(jnp.int32, (total, total), 0)
    col_ids = lax.broadcasted_iota(jnp.int32, (total, total), 1)
    inverse_ref[...] = jnp.where(row_ids == col_ids, 1.0, 0.0)
    for k in range(blocks):
        own = slice(k * BLOCK, (k + 1) * BLOCK)
        done = (k + 1) * BLOCK
        small = halves(block_inverse(work[own, own]))
        head = three_dot(small, halves(inverse_ref[own, :done]), 1, 0)
        inverse_ref[own, :done] = head
        if done < total:
            panel = halves(three_dot(halves(work[done:, own]), small, 1, 1))
            work[done:, done:] = work[done:, done:] - three_dot(panel, panel, 1, 1)
            inverse_ref[done:, :done] = inverse_ref[done:, :done] - three_dot(panel, halves(head), 1, 0)


def factor_inverse(matrix):
    return pl.pallas_call(
        inverse_kernel,
        out_shape=jax.ShapeDtypeStruct(matrix.shape, jnp.float32),
        in_specs=[pl.BlockSpec(memory_space=pltpu.VMEM)],
        out_specs=pl.BlockSpec(memory_space=pltpu.VMEM),
        scratch_shapes=[pltpu.VMEM(matrix.shape, jnp.float32)],
        compiler_params=pltpu.CompilerParams(vmem_limit_bytes=40 * 1024 * 1024),
        cost_estimate=pl.CostEstimate(flops=2 * 10**10, bytes_accessed=5 * 10**6, transcendentals=0),
    )(matrix)


def body(points, targets, centres):
    everyone = lax.all_gather(centres, "ctr", axis=0, tiled=True)
    norms = square_norms(everyone)
    count = everyone.shape[0]
    total_points = points.shape[0] * lax.axis_size("pts")
    scaling = 1.0 / math.sqrt(total_points)
    share = points.shape[0] // lax.axis_size("ctr")
    own_start = lax.axis_index("ctr") * share
    own_points = lax.dynamic_slice_in_dim(points, own_start, share, 0)
    own_targets = lax.dynamic_slice_in_dim(targets, own_start, share, 0)
    own_kernel = kernel_block(own_points, everyone, norms)
    partial = split_dot(own_kernel.T, jnp.concatenate([own_kernel, own_targets], axis=1))
    summed = lax.psum(partial, ("pts", "ctr"))

    gram = kernel_block(everyone, everyone, norms)
    inverse = factor_inverse(split_dot(gram, gram) / count + PENALTY * gram)
    normal = summed[:, :count] * (1.0 / total_points) + PENALTY * gram
    residual = split_dot(inverse, summed[:, count:] * scaling)
    direction = residual
    solution = jnp.zeros(residual.shape, jnp.float32)
    sq_now = jnp.sum(residual * residual, axis=0)
    for iteration in range(ITERS):
        image = split_dot(inverse, split_dot(normal, split_dot(inverse.T, direction)))
        step_size = sq_now / jnp.sum(direction * image, axis=0)
        solution = solution + step_size * direction
        residual = residual - step_size * image
        sq_next = jnp.sum(residual * residual, axis=0)
        direction = residual + sq_next / sq_now * direction
        sq_now = sq_next
    weights = split_dot(inverse.T, solution) * scaling
    fitted = split_dot(kernel_block(points, everyone, norms), weights)
    per_device = centres.shape[0]
    own_solution = lax.dynamic_slice_in_dim(solution, lax.axis_index("ctr") * per_device, per_device, 0)
    return (own_solution, fitted)


def solution(mesh):
    return jax.shard_map(
        body,
        mesh=mesh,
        in_specs=(
            P(("groups", "pts"), None),
            P(("groups", "pts"), None),
            P(("groups", "ctr"), None),
        ),
        out_specs=(P(("groups", "ctr"), None), P(("groups", "pts"), None)),
        check_vma=False,
    )
```

```python
import functools
import math

import jax
import jax.numpy as jnp
from jax import lax
from jax.experimental import pallas as pl
from jax.experimental.pallas import tpu as pltpu
from jax.sharding import PartitionSpec as P

ITERS = 3
GAMMA = 3.0
PENALTY = 0.001
BLOCK = 128
PANEL = 8


def square_norms(row_set):
    widened = row_set.astype(jnp.float32)
    return jnp.sum(widened * widened, axis=1)


def kernel_tile(rows, centres, centre_norms):
    inner_prod = lax.dot_general(rows, centres, (((1,), (1,)), ((), ())), preferred_element_type=jnp.float32)
    widened = rows.astype(jnp.float32)
    row_norms = jnp.sum(widened * widened, axis=1, keepdims=True)
    return jnp.exp(-GAMMA * (row_norms + centre_norms - 2.0 * inner_prod))


def halves(value):
    high = value.astype(jnp.bfloat16)
    return high, (value - high.astype(jnp.float32)).astype(jnp.bfloat16)


def three_dot(left, right, left_dim, right_dim):
    dims = (((left_dim,), (right_dim,)), ((), ()))

    def one(a, b):
        return lax.dot_general(a, b, dims, preferred_element_type=jnp.float32)

    return one(left[0], right[0]) + (one(left[0], right[1]) + one(left[1], right[0]))


def block_inverse(mixed):
    size = mixed.shape[0]
    lanes = lax.broadcasted_iota(jnp.int32, (PANEL, size), 1)
    rows = lax.broadcasted_iota(jnp.int32, (PANEL, size), 0)
    finished = []
    rest = mixed
    for start in range(0, size, PANEL):
        panel = rest[:PANEL]
        below = rest[PANEL:]
        count = below.shape[0]
        cols = [
            jnp.broadcast_to(panel[:, start + c : start + c + 1], (PANEL, size)) for c in range(PANEL)
        ]
        if count:
            lows = [
                jnp.broadcast_to(below[:, start + c : start + c + 1], (count, size)) for c in range(PANEL)
            ]
            below_lanes = lax.broadcasted_iota(jnp.int32, (count, size), 1)
            inside = (below_lanes >= start) & (below_lanes < start + PANEL)
            below = jnp.where(inside, 0.0, below)
        inside_panel = (lanes >= start) & (lanes < start + PANEL)
        panel = jnp.where(inside_panel, jnp.where(lanes - start == rows, 1.0, 0.0), panel)
        for c in range(PANEL):
            root = lax.rsqrt(cols[c][c : c + 1])
            scaled = panel[c : c + 1] * root
            lower = jnp.where(rows > c, cols[c] * root, 0.0)
            panel = jnp.where(rows == c, scaled, panel - lower * scaled)
            if count:
                low = lows[c] * root
                below = below - low * scaled
            for later in range(c + 1, PANEL):
                factor = cols[later][c : c + 1] * root
                cols[later] = cols[later] - lower * factor
                if count:
                    lows[later] = lows[later] - low * factor
        finished.append(jnp.where(lanes < start + PANEL, panel, 0.0))
        rest = below
    return jnp.concatenate(finished, axis=0)


def put(pair_refs, where, value):
    pair_refs[0][where], pair_refs[1][where] = halves(value)


def lower_place(i, blocks):
    half = blocks // 2
    if i >= half:
        return slice((blocks - 1 - i) * BLOCK, (blocks - i) * BLOCK), 0
    return slice(i * BLOCK, (i + 1) * BLOCK), (blocks - i) * BLOCK


def target_place(i, blocks, outs):
    half = blocks // 2
    first = (blocks + 1) * BLOCK + (i // half) * outs
    return slice((i % half) * BLOCK, (i % half + 1) * BLOCK), slice(first, first + outs)


def products_kernel(points_ref, targets_ref, centres_ref, norms_ref, out_ref, high, low):
    count = centres_ref.shape[0]
    rows = points_ref.shape[0]
    outs = targets_ref.shape[1]
    blocks = count // BLOCK
    step = min(256, rows)
    for start in range(0, rows, step):
        where = slice(start, start + step)
        put((high, low), where, kernel_tile(points_ref[where], centres_ref[...], norms_ref[...]))
    target_pair = halves(targets_ref[...])
    for pair in range(blocks // 2):
        own = slice(2 * pair * BLOCK, 2 * (pair + 1) * BLOCK)
        left = (high[:, own], low[:, own])
        done = own.stop
        value = three_dot(left, (high[:, :done], low[:, :done]), 0, 0)
        labels = three_dot(left, target_pair, 0, 0)
        for part in range(2):
            i = 2 * pair + part
            inside = slice(part * BLOCK, (part + 1) * BLOCK)
            place, first = lower_place(i, blocks)
            out_ref[place, first : first + (i + 1) * BLOCK] = value[inside, : (i + 1) * BLOCK]
            place, lanes = target_place(i, blocks, outs)
            out_ref[place, lanes] = labels[inside]


def factor_kernel(
    points_ref, centres_ref, norms_ref, columns_ref, gram_ref, high_ref, low_ref, turned_high_ref, turned_low_ref,
    kernel_high_ref, kernel_low_ref, work, inverse, pair_high, pair_low
):
    total = centres_ref.shape[0]
    blocks = total // BLOCK
    inner_prod = lax.dot_general(
        centres_ref[...], centres_ref[...], (((1,), (1,)), ((), ())), preferred_element_type=jnp.float32
    )
    gram = jnp.exp(-GAMMA * (columns_ref[...] + norms_ref[...] - 2.0 * inner_prod))
    gram_ref[...] = gram
    put((pair_high, pair_low), slice(None), gram)
    pair = (pair_high[...], pair_low[...])
    work[...] = three_dot(pair, pair, 1, 0) * (1.0 / total) + PENALTY * gram_ref[...]
    row_ids = lax.broadcasted_iota(jnp.int32, (total, total), 0)
    col_ids = lax.broadcasted_iota(jnp.int32, (total, total), 1)
    inverse[...] = jnp.where(row_ids == col_ids, 1.0, 0.0)
    for k in range(blocks):
        own = slice(k * BLOCK, (k + 1) * BLOCK)
        done = (k + 1) * BLOCK
        small = halves(block_inverse(work[own, own]))
        head = three_dot(small, halves(inverse[own, :done]), 1, 0)
        inverse[own, :done] = head
        if done < total:
            panel = halves(three_dot(halves(work[done:, own]), small, 1, 1))
            work[done:, done:] = work[done:, done:] - three_dot(panel, panel, 1, 1)
            inverse[done:, :done] = inverse[done:, :done] - three_dot(panel, halves(head), 1, 0)
    put((high_ref, low_ref), slice(None), inverse[...])
    put((turned_high_ref, turned_low_ref), slice(None), inverse[...].T)
    step = min(256, points_ref.shape[0])
    for start in range(0, points_ref.shape[0], step):
        where = slice(start, start + step)
        put((kernel_high_ref, kernel_low_ref), where, kernel_tile(points_ref[where], centres_ref[...], norms_ref[...]))


def iterate_kernel(
    total_points, packed_ref, gram_ref, high_ref, low_ref, turned_high_ref, turned_low_ref, kernel_high_ref,
    kernel_low_ref, solution_ref, fitted_ref, normal_high, normal_low, kernel_high, kernel_low, arrived
):
    copies = [
        pltpu.make_async_copy(kernel_high_ref, kernel_high, arrived.at[0]),
        pltpu.make_async_copy(kernel_low_ref, kernel_low, arrived.at[1]),
    ]
    for copy in copies:
        copy.start()
    total, outs = solution_ref.shape
    blocks = total // BLOCK
    scaling = 1.0 / math.sqrt(total_points)
    labels = []
    for i in range(blocks):
        own = slice(i * BLOCK, (i + 1) * BLOCK)
        place, first = lower_place(i, blocks)
        for j in range(i + 1):
            other = slice(j * BLOCK, (j + 1) * BLOCK)
            lanes = slice(first + j * BLOCK, first + (j + 1) * BLOCK)
            value = packed_ref[place, lanes] * (1.0 / total_points) + PENALTY * gram_ref[own, other]
            put((normal_high, normal_low), (own, other), value)
            if j < i:
                put((normal_high, normal_low), (other, own), value.T)
        place, lanes = target_place(i, blocks, outs)
        labels.append(packed_ref[place, lanes])

    def apply(high, low, value):
        return three_dot((high[...], low[...]), halves(value), 1, 0)

    residual = apply(high_ref, low_ref, jnp.concatenate(labels, axis=0) * scaling)
    direction = residual
    result = jnp.zeros_like(residual)
    sq_now = jnp.sum(residual * residual, axis=0, keepdims=True)
    for iteration in range(ITERS):
        right = apply(turned_high_ref, turned_low_ref, direction)
        image = apply(high_ref, low_ref, apply(normal_high, normal_low, right))
        step_size = sq_now / jnp.sum(direction * image, axis=0, keepdims=True)
        result = result + step_size * direction
        residual = residual - step_size * image
        sq_next = jnp.sum(residual * residual, axis=0, keepdims=True)
        direction = residual + sq_next / sq_now * direction
        sq_now = sq_next
    solution_ref[...] = result
    weights = apply(turned_high_ref, turned_low_ref, result) * scaling
    for copy in copies:
        copy.wait()
    fitted_ref[...] = apply(kernel_high, kernel_low, weights)


def call(kernel, ins, outs, scratch, flops, arguments):
    space = pl.BlockSpec(memory_space=pltpu.VMEM)
    return pl.pallas_call(
        kernel,
        out_shape=outs,
        in_specs=[space if vmem else pl.BlockSpec(memory_space=pl.ANY) for vmem in ins],
        out_specs=jax.tree.map(lambda _: space, outs),
        scratch_shapes=scratch,
        compiler_params=pltpu.CompilerParams(vmem_limit_bytes=48 * 1024 * 1024),
        cost_estimate=pl.CostEstimate(flops=flops, bytes_accessed=10**7, transcendentals=0),
    )(*arguments)


def body(points, targets, centres):
    everyone = lax.all_gather(centres, "ctr", axis=0, tiled=True)
    norms = square_norms(everyone)
    norm_row = norms[None, :]
    count, outs = everyone.shape[0], targets.shape[1]
    rows = points.shape[0]
    total_points = rows * lax.axis_size("pts")
    share = rows // lax.axis_size("ctr")
    own_start = lax.axis_index("ctr") * share
    own_points = lax.dynamic_slice_in_dim(points, own_start, share, 0)
    own_targets = lax.dynamic_slice_in_dim(targets, own_start, share, 0)
    shape = jax.ShapeDtypeStruct
    width = count + BLOCK + 2 * outs
    partial = call(
        products_kernel,
        [True] * 4,
        shape((count // 2, width), jnp.float32),
        [pltpu.VMEM((share, count), jnp.bfloat16)] * 2,
        4 * 10**9,
        (own_points, own_targets, everyone, norm_row),
    )
    packed = lax.psum(partial, ("pts", "ctr"))
    square, tall = shape((count, count), jnp.bfloat16), shape((rows, count), jnp.bfloat16)
    made = call(
        factor_kernel,
        [True] * 4,
        [shape((count, count), jnp.float32)] + [square] * 4 + [tall] * 2,
        [pltpu.VMEM((count, count), jnp.float32)] * 2 + [pltpu.VMEM((count, count), jnp.bfloat16)] * 2,
        3 * 10**10,
        (points, everyone, norm_row, norms[:, None]),
    )
    result, fitted = call(
        functools.partial(iterate_kernel, total_points),
        [True] * 6 + [False] * 2,
        [shape((count, outs), jnp.float32), shape((rows, outs), jnp.float32)],
        [pltpu.VMEM((count, count), jnp.bfloat16)] * 2
        + [pltpu.VMEM((rows, count), jnp.bfloat16)] * 2
        + [pltpu.SemaphoreType.DMA((2,))],
        6 * 10**9,
        (packed, *made),
    )
    per_device = centres.shape[0]
    own_solution = lax.dynamic_slice_in_dim(result, lax.axis_index("ctr") * per_device, per_device, 0)
    return (own_solution, fitted)


def solution(mesh):
    return jax.shard_map(
        body,
        mesh=mesh,
        in_specs=(
            P(("groups", "pts"), None),
            P(("groups", "pts"), None),
            P(("groups", "ctr"), None),
        ),
        out_specs=(P(("groups", "ctr"), None), P(("groups", "pts"), None)),
        check_vma=False,
    )
```

```python
import math

import jax
import jax.numpy as jnp
from jax import lax
from jax.experimental import pallas as pl
from jax.experimental.pallas import tpu as pltpu
from jax.sharding import PartitionSpec as P

ITERS = 3
GAMMA = 3.0
PENALTY = 0.001
BLOCK = 128
PANEL = 8


def split_dot(left, right):
    return jnp.dot(left, right, precision=lax.Precision.HIGH, preferred_element_type=jnp.float32)


def square_norms(row_set):
    widened = row_set.astype(jnp.float32)
    return jnp.sum(widened * widened, axis=1)


def kernel_block(row_set, col_set, col_norms):
    inner_prod = jnp.dot(row_set, col_set.T, preferred_element_type=jnp.float32)
    row_norms = square_norms(row_set)
    return jnp.exp(-GAMMA * (row_norms[:, None] + col_norms[None, :] - 2.0 * inner_prod))


def halves(value):
    high = value.astype(jnp.bfloat16)
    return high, (value - high.astype(jnp.float32)).astype(jnp.bfloat16)


def three_dot(left, right, left_dim, right_dim):
    dims = (((left_dim,), (right_dim,)), ((), ()))

    def one(a, b):
        return lax.dot_general(a, b, dims, preferred_element_type=jnp.float32)

    return one(left[0], right[0]) + (one(left[0], right[1]) + one(left[1], right[0]))


def block_inverse(mixed):
    size = mixed.shape[0]
    lanes = lax.broadcasted_iota(jnp.int32, (PANEL, size), 1)
    rows = lax.broadcasted_iota(jnp.int32, (PANEL, size), 0)
    finished = []
    rest = mixed
    for start in range(0, size, PANEL):
        panel = rest[:PANEL]
        below = rest[PANEL:]
        count = below.shape[0]
        cols = [
            jnp.broadcast_to(panel[:, start + c : start + c + 1], (PANEL, size)) for c in range(PANEL)
        ]
        if count:
            lows = [
                jnp.broadcast_to(below[:, start + c : start + c + 1], (count, size)) for c in range(PANEL)
            ]
            below_lanes = lax.broadcasted_iota(jnp.int32, (count, size), 1)
            inside = (below_lanes >= start) & (below_lanes < start + PANEL)
            below = jnp.where(inside, 0.0, below)
        inside_panel = (lanes >= start) & (lanes < start + PANEL)
        panel = jnp.where(inside_panel, jnp.where(lanes - start == rows, 1.0, 0.0), panel)
        for c in range(PANEL):
            root = lax.rsqrt(cols[c][c : c + 1])
            scaled = panel[c : c + 1] * root
            lower = jnp.where(rows > c, cols[c] * root, 0.0)
            panel = jnp.where(rows == c, scaled, panel - lower * scaled)
            if count:
                low = lows[c] * root
                below = below - low * scaled
            for later in range(c + 1, PANEL):
                factor = cols[later][c : c + 1] * root
                cols[later] = cols[later] - lower * factor
                if count:
                    lows[later] = lows[later] - low * factor
        finished.append(jnp.where(lanes < start + PANEL, panel, 0.0))
        rest = below
    return jnp.concatenate(finished, axis=0)


def inverse_kernel(matrix_ref, inverse_ref, work):
    total = matrix_ref.shape[0]
    blocks = total // BLOCK
    work[...] = matrix_ref[...]
    row_ids = lax.broadcasted_iota(jnp.int32, (total, total), 0)
    col_ids = lax.broadcasted_iota(jnp.int32, (total, total), 1)
    inverse_ref[...] = jnp.where(row_ids == col_ids, 1.0, 0.0)
    for k in range(blocks):
        own = slice(k * BLOCK, (k + 1) * BLOCK)
        done = (k + 1) * BLOCK
        small = halves(block_inverse(work[own, own]))
        head = three_dot(small, halves(inverse_ref[own, :done]), 1, 0)
        inverse_ref[own, :done] = head
        if done < total:
            panel = halves(three_dot(halves(work[done:, own]), small, 1, 1))
            work[done:, done:] = work[done:, done:] - three_dot(panel, panel, 1, 1)
            inverse_ref[done:, :done] = inverse_ref[done:, :done] - three_dot(panel, halves(head), 1, 0)


def factor_inverse(matrix):
    return pl.pallas_call(
        inverse_kernel,
        out_shape=jax.ShapeDtypeStruct(matrix.shape, jnp.float32),
        in_specs=[pl.BlockSpec(memory_space=pltpu.VMEM)],
        out_specs=pl.BlockSpec(memory_space=pltpu.VMEM),
        scratch_shapes=[pltpu.VMEM(matrix.shape, jnp.float32)],
        compiler_params=pltpu.CompilerParams(vmem_limit_bytes=40 * 1024 * 1024),
        cost_estimate=pl.CostEstimate(flops=2 * 10**10, bytes_accessed=5 * 10**6, transcendentals=0),
    )(matrix)


def body(points, targets, centres):
    everyone = lax.all_gather(centres, "ctr", axis=0, tiled=True)
    norms = square_norms(everyone)
    count = everyone.shape[0]
    total_points = points.shape[0] * lax.axis_size("pts")
    scaling = 1.0 / math.sqrt(total_points)
    all_kernel = kernel_block(points, everyone, norms)
    own_kernel = kernel_block(points, centres, square_norms(centres))
    partial = split_dot(own_kernel.T, jnp.concatenate([all_kernel, targets], axis=1))
    own_rows = lax.psum(partial, "pts")

    gram = kernel_block(everyone, everyone, norms)
    inverse = factor_inverse(split_dot(gram, gram) / count + PENALTY * gram)
    summed = lax.all_gather(own_rows, "ctr", axis=0, tiled=True)
    normal = summed[:, :count] * (1.0 / total_points) + PENALTY * gram
    residual = split_dot(inverse, summed[:, count:] * scaling)
    direction = residual
    solution = jnp.zeros(residual.shape, jnp.float32)
    sq_now = jnp.sum(residual * residual, axis=0)
    for iteration in range(ITERS):
        image = split_dot(inverse, split_dot(normal, split_dot(inverse.T, direction)))
        step_size = sq_now / jnp.sum(direction * image, axis=0)
        solution = solution + step_size * direction
        residual = residual - step_size * image
        sq_next = jnp.sum(residual * residual, axis=0)
        direction = residual + sq_next / sq_now * direction
        sq_now = sq_next
    weights = split_dot(inverse.T, solution) * scaling
    fitted = split_dot(all_kernel, weights)
    per_device = centres.shape[0]
    own_solution = lax.dynamic_slice_in_dim(solution, lax.axis_index("ctr") * per_device, per_device, 0)
    return (own_solution, fitted)


def solution(mesh):
    return jax.shard_map(
        body,
        mesh=mesh,
        in_specs=(
            P(("groups", "pts"), None),
            P(("groups", "pts"), None),
            P(("groups", "ctr"), None),
        ),
        out_specs=(P(("groups", "ctr"), None), P(("groups", "pts"), None)),
        check_vma=False,
    )
```
